512 devices in a mesh: src: 16 (over y, z_hi), tgt: 32 (over z_lo, x, core).
Axes of the slice: x: 4, y: 8, z: 8 (z_hi: 2, z_lo: 4; z = z_hi * 4 + z_lo), core: 2. Of those that a mesh axis runs over, the one named last changes fastest.
Arguments:
- source_points: float32 [4096, 384], P('src'), as said below
- target_points: float32 [24576, 384], P('tgt'), as said below
- plan_start: float32 [4096, 24576], P('src', 'tgt'), may hold values from 0.06 to 140, as said below
- source_mass: float32 [4096], P('src'), may hold values from 0.3 to 3
- target_mass: float32 [24576], P('tgt'), may hold values from 0.3 to 3
- epsilon: float32 [1], replicated, may hold values from 0.5 to 1
Outputs:
- transported: float32 [4096, 384], P(('src', 'tgt'))
- core: float32 [384, 384], replicated
- column_scale: float32 [24576], P('tgt')
The draws below stay inside these ranges and needn't reach their ends.
Inputs may be any that keep to these rules, and one draw needn't show every extreme that they name: `source_points`: real-valued features. `target_points`: real-valued features. `plan_start`: positive entries.
All inputs are finite; a program needn't handle non-finite values.
Results may differ from the reference program's by a relative error of at most 0.00011.
Values sent between devices are 32-bit elements; how exact they have to be, the bound alone decides.
A program may use at most 64 MiB of HBM per device.

```python
import math
import jax
import jax.numpy as jnp
from jax import lax

D = 384
ITERS = 2
SOURCES = 4096
TARGETS = 24576


def shared_fields(key):
    base = jax.random.fold_in(key, 7101)
    keys = jax.random.split(base, 7)
    latent_src = jnp.clip(jax.random.normal(keys[0], (SOURCES, D), jnp.float32), -3.0, 3.0)
    latent_tgt = jnp.clip(jax.random.normal(keys[1], (TARGETS, D), jnp.float32), -3.0, 3.0)
    mixing_src = jnp.eye(D, dtype=jnp.float32) + 0.6 * jax.random.normal(keys[2], (D, D), jnp.float32) / math.sqrt(1.0 * D)
    mixing_tgt = jnp.eye(D, dtype=jnp.float32) + 0.6 * jax.random.normal(keys[3], (D, D), jnp.float32) / math.sqrt(1.0 * D)
    points_src = 0.5 * jnp.dot(latent_src, mixing_src)
    points_tgt = 0.5 * jnp.dot(latent_tgt, mixing_tgt)
    similar = jnp.clip(jnp.dot(latent_src, latent_tgt.T) / math.sqrt(1.0 * D), -4.0, 4.0)
    rough = jnp.exp(jax.random.uniform(keys[6], (SOURCES, TARGETS), jnp.float32, math.log(0.5), math.log(2.0)))
    row_rise = jnp.exp(math.log(3.0) * jnp.arange(SOURCES, dtype=jnp.float32) / SOURCES)
    col_rise = jnp.exp(math.log(3.0) * jnp.arange(TARGETS, dtype=jnp.float32) / TARGETS)
    plan = rough * jnp.exp(0.5 * similar) * row_rise[:, None] * col_rise[None, :]
    return (points_src, points_tgt, plan)


def draw_source_points(key, part):
    return shared_fields(key)[0]


def draw_target_points(key, part):
    return shared_fields(key)[1]


def draw_plan_start(key, part):
    return shared_fields(key)[2]


def shard_levels(key, shape, pieces, low, top_value):
    factor_of = 1.0
    for axis_at, blocks in pieces:
        draws = jax.random.uniform(jax.random.fold_in(jax.random.fold_in(key, 6), axis_at), (blocks,), jnp.float32, low / len(pieces), top_value / len(pieces))
        factor_of = factor_of * jnp.repeat(jnp.exp(draws), shape[axis_at] // blocks).reshape((-1,) + (1,) * (len(shape) - 1 - axis_at))
    return factor_of


def setup_inputs(seed: int = 0) -> dict:
    key_list = jax.random.split(jax.random.key(seed), 7)
    source_points = draw_source_points(jax.random.fold_in(key_list[6], 71), 0)
    target_points = draw_target_points(jax.random.fold_in(key_list[6], 71), 0)
    plan_start = draw_plan_start(jax.random.fold_in(key_list[6], 71), 0)
    source_mass = jnp.clip(jnp.exp(math.log(3.0) - 2.3025851 * jax.random.uniform(key_list[3], (SOURCES,), jnp.float32) ** shard_levels(key_list[3], (SOURCES,), ((0, 16),), -0.2, 0.2)), 0.3, 3.0)
    target_mass = jnp.clip(jnp.exp(math.log(3.0) - 2.3025851 * jax.random.uniform(key_list[4], (TARGETS,), jnp.float32) ** shard_levels(key_list[4], (TARGETS,), ((0, 32),), -0.2, 0.2)), 0.3, 3.0)
    epsilon = jnp.clip(jax.random.uniform(key_list[5], (1,), jnp.float32, 0.5, 1.0), 0.5, 1.0)
    return dict(source_points=source_points, target_points=target_points, plan_start=plan_start, source_mass=source_mass, target_mass=target_mass, epsilon=epsilon)


def product(left, right):
    return jnp.dot(left, right, precision=lax.Precision.HIGHEST, preferred_element_type=jnp.float32)


def reference(source_points, target_points, plan_start, source_mass, target_mass, epsilon):
    moved = product(plan_start, target_points)
    core = product(source_points.T, moved) / (SOURCES * TARGETS)
    affinity = product(product(source_points, core), target_points.T)
    kernel = plan_start * jnp.exp(2.0 * affinity / epsilon[0])
    column_scale = jnp.ones((TARGETS,), jnp.float32)
    row_scale = jnp.ones((SOURCES,), jnp.float32)
    for sweep in range(ITERS):
        row_scale = source_mass / product(kernel, column_scale)
        column_scale = target_mass / product(row_scale, kernel)
    weighted = kernel * row_scale[:, None] * column_scale[None, :]
    transported = product(weighted, target_points) / source_mass[:, None]
    return transported, core, column_scale
```

```python
import functools

import jax
import jax.numpy as jnp
from jax import lax
from jax.experimental import pallas as pl
from jax.experimental.pallas import tpu as pltpu
from jax.sharding import PartitionSpec as P

MESH = pl.DeviceIdType.MESH
D = 384
ROWS = 256
COLS = 768
SLAB = 12
TOTAL = 4096 * 24576

PAIR = (0, 1)


def near_mask(d):
    return (((d >> 2) & 1) << 1, ((d & 3) << 1) | (((d >> 3) & 1) << 3))


def wide_mask(e):
    return (((e & 3) << 2) | ((e >> 3) & 1), ((e >> 2) & 1) << 4)


def place(s, t):
    return (t // 2 % 4, s // 2, (s % 2) * 4 + t // 8)


def ring(a, b, n):
    return min(abs(a - b), n - abs(a - b))


def hops(mask):
    most = 0
    for s in range(16):
        for t in range(32):
            a, b = place(s, t), place(s ^ mask[0], t ^ mask[1])
            most = max(most, ring(a[0], b[0], 4) + ring(a[1], b[1], 8) + ring(a[2], b[2], 8))
    return most


def far_first(masks):
    return sorted(range(1, len(masks)), key=lambda d: -hops(masks[d]))


NEAR = [near_mask(d) for d in range(16)]
WIDE = [wide_mask(d) for d in range(16)]
TGT = [(0, d) for d in range(32)]
SRC = [(d, 0) for d in range(16)]
TILE = [(0, 2 * d) for d in range(16)]
NEAR_ORDER, WIDE_ORDER, TGT_ORDER, SRC_ORDER, TILE_ORDER = map(far_first, (NEAR, WIDE, TGT, SRC, TILE))
GREET = sorted({PAIR, *NEAR[1:], *WIDE[1:], *TGT[1:], *SRC[1:]})


def bits_of(value, n):
    return [lax.rem(lax.div(value, 1 << k), 2) for k in range(n)]


def flipped(value, bits, mask):
    for k, bit in enumerate(bits):
        if (mask >> k) & 1:
            value = value + (1 << k) * (1 - 2 * bit)
    return value


def dot(a, b, contract=((1,), (0,))):
    return lax.dot_general(
        a, b, (contract, ((), ())), precision=lax.Precision.HIGHEST, preferred_element_type=jnp.float32
    )


def body(
    s_ref, t_ref, p_ref, a_ref, b_ref, eps_ref,
    out_ref, core_ref, col_ref,
    st, half, pair_in, acc, near_in, wide, gathered, kern, row_in, col_in, part, part_in, mine, last_in,
    send, recv,
):
    si, ti = lax.axis_index("src"), lax.axis_index("tgt")
    sb, tb = bits_of(si, 4), bits_of(ti, 5)
    core = tb[0]
    g = tb[1] + 2 * tb[2] + 4 * sb[1] + 8 * tb[3]
    gb = [tb[1], tb[2], sb[1], tb[3]]
    w = sb[2] + 2 * sb[3] + 4 * tb[4] + 8 * sb[0]
    tile = tb[1] + 2 * tb[2] + 4 * tb[3] + 8 * tb[4]
    tileb = tb[1:]

    def device(mask):
        return (flipped(si, sb, mask[0]), flipped(ti, tb, mask[1]))

    def copy(src, dst, k, mask):
        return pltpu.make_async_remote_copy(
            src, dst, send.at[k], recv.at[k], device_id=device(mask), device_id_type=MESH
        )

    def arrived(ref, k):
        copy(ref, ref, k, PAIR).wait_recv()

    def sent(ref, k):
        copy(ref, ref, k, PAIR).wait_send()

    barrier = pltpu.get_barrier_semaphore()
    for mask in GREET:
        pl.semaphore_signal(barrier, inc=1, device_id=device(mask), device_id_type=MESH)

    st[...] = s_ref[...].T
    moved = dot(p_ref[...], t_ref[...])
    for k, h in ((0, 1 - core), (1, core)):
        value = dot(st[pl.ds(pl.multiple_of(h * 192, 8), 192), :], moved)
        for q in range(16):
            half[k, q] = value[q * SLAB : (q + 1) * SLAB]
        if k == 0:
            pl.semaphore_wait(barrier, len(GREET))
            copy(half.at[0], pair_in, 0, PAIR).start()
    arrived(pair_in, 0)
    acc[...] = half[1] + pair_in[...]

    for d in NEAR_ORDER:
        copy(acc.at[flipped(g, gb, d)], near_in.at[d - 1], 1, NEAR[d]).start()
    arrived(near_in, 1)
    total = acc[g]
    for d in range(15):
        total = total + near_in[d]
    wide[w] = total

    for d in WIDE_ORDER:
        copy(wide.at[w], wide.at[w], 2, WIDE[d]).start()
    arrived(wide.at[pl.ds(0, 15)], 2)
    total = wide[0]
    for d in range(1, 16):
        total = total + wide[d]
    gathered[core, g] = total / TOTAL

    for d in NEAR_ORDER:
        copy(gathered.at[core, g], gathered.at[core, g], 3, NEAR[d]).start()
    arrived(gathered.at[0, pl.ds(0, 15)], 3)
    copy(gathered.at[core], gathered.at[core], 4, PAIR).start()
    arrived(gathered.at[0], 4)
    for q in range(32):
        core_ref[q * SLAB : (q + 1) * SLAB, :] = gathered[q // 16, q % 16]

    rate = 2.0 / eps_ref[0]
    left = dot(s_ref[...], core_ref[...]) * rate
    kern[...] = p_ref[...] * jnp.exp(dot(left, t_ref[...], ((1,), (1,))))

    def settle(x):
        x = x + pltpu.roll(x, 4, 0)
        x = x + pltpu.roll(x, 2, 0)
        return x + pltpu.roll(x, 1, 0)

    def row_total(scale, k, n):
        parts = None
        for j in range(COLS // 128):
            piece = kern[:, j * 128 : (j + 1) * 128]
            if scale is not None:
                piece = piece * scale[0:1, j * 128 : (j + 1) * 128]
            parts = piece if parts is None else parts + piece
        across = parts.T
        x = across[0:8]
        for j in range(1, 16):
            x = x + across[j * 8 : (j + 1) * 8]
        row_in[n, 0] = settle(x)[0:1]
        for d in TGT_ORDER:
            copy(row_in.at[n, 0], row_in.at[n, d], k, TGT[d]).start()
        arrived(row_in.at[n, pl.ds(0, 31)], k)
        x = row_in[n, 0]
        for d in range(1, 32):
            x = x + row_in[n, d]
        return x

    def col_total(k, n):
        x = kern[0:8, :] * down[0:8, 0:1] if n == 0 else kern[0:8, :]
        for j in range(1, 32):
            piece = kern[j * 8 : (j + 1) * 8, :]
            x = x + (piece * down[j * 8 : (j + 1) * 8, 0:1] if n == 0 else piece)
        col_in[n, si] = settle(x)[0:1]
        for d in SRC_ORDER:
            copy(col_in.at[n, si], col_in.at[n, si], k, SRC[d]).start()
        arrived(col_in.at[n, pl.ds(0, 15)], k)
        x = col_in[n, 0]
        for d in range(1, 16):
            x = x + col_in[n, d]
        return x

    scale = None
    for n in range(2):
        row = a_ref[...] / row_total(scale, 5 + 2 * n, n)
        down = jnp.broadcast_to(row, (128, ROWS)).T
        if n == 1:
            kern[...] = kern[...] * down[:, 0:1]
        scale = b_ref[...] / col_total(6 + 2 * n, n)
    col_ref[...] = scale[0:1]

    value = dot(kern[...] * scale[0:1], t_ref[...])
    for q in range(32):
        part[q % 2, q // 2] = value[q * 8 : (q + 1) * 8]
    copy(part.at[1 - core], part_in, 9, PAIR).start()
    arrived(part_in, 9)
    mine[...] = part[core] + part_in[...]
    for d in TILE_ORDER:
        copy(mine.at[flipped(tile, tileb, d)], last_in.at[d - 1], 10, TILE[d]).start()
    arrived(last_in, 10)
    total = mine[tile]
    for d in range(15):
        total = total + last_in[d]
    out_ref[...] = total

    sent(half.at[0], 0)
    sent(near_in, 1)
    sent(wide.at[pl.ds(0, 15)], 2)
    sent(gathered.at[0, pl.ds(0, 15)], 3)
    sent(gathered.at[0], 4)
    for n in range(2):
        sent(row_in.at[n, pl.ds(0, 31)], 5 + 2 * n)
        sent(col_in.at[n, pl.ds(0, 15)], 6 + 2 * n)
    sent(part_in, 9)
    sent(last_in, 10)


def per_device(source_points, target_points, plan_start, source_mass, target_mass, epsilon):
    f32 = jnp.float32
    vmem = pl.BlockSpec(memory_space=pltpu.VMEM)
    out, core, col = pl.pallas_call(
        body,
        out_shape=(
            jax.ShapeDtypeStruct((8, D), f32),
            jax.ShapeDtypeStruct((D, D), f32),
            jax.ShapeDtypeStruct((1, COLS), f32),
        ),
        in_specs=[vmem] * 5 + [pl.BlockSpec(memory_space=pltpu.SMEM)],
        out_specs=(vmem, vmem, vmem),
        scratch_shapes=[
            pltpu.VMEM((D, ROWS), f32),
            pltpu.VMEM((2, 16, SLAB, D), f32),
            pltpu.VMEM((16, SLAB, D), f32),
            pltpu.VMEM((16, SLAB, D), f32),
            pltpu.VMEM((15, SLAB, D), f32),
            pltpu.VMEM((16, SLAB, D), f32),
            pltpu.VMEM((2, 16, SLAB, D), f32),
            pltpu.VMEM((ROWS, COLS), f32),
            pltpu.VMEM((2, 32, 1, ROWS), f32),
            pltpu.VMEM((2, 16, 1, COLS), f32),
            pltpu.VMEM((2, 16, 8, D), f32),
            pltpu.VMEM((16, 8, D), f32),
            pltpu.VMEM((16, 8, D), f32),
            pltpu.VMEM((15, 8, D), f32),
            pltpu.SemaphoreType.DMA((11,)),
            pltpu.SemaphoreType.DMA((11,)),
        ],
        compiler_params=pltpu.CompilerParams(
            collective_id=0, has_side_effects=True, vmem_limit_bytes=48 * 2**20
        ),
    )(
        source_points, target_points, plan_start,
        source_mass.reshape(1, ROWS), target_mass.reshape(1, COLS), epsilon,
    )
    mass = lax.dynamic_slice(source_mass, (8 * lax.axis_index("tgt"),), (8,))
    return out / mass[:, None], core, col.reshape(COLS)


def solution(mesh):
    return jax.shard_map(
        per_device,
        mesh=mesh,
        in_specs=(P("src", None), P("tgt", None), P("src", "tgt"), P("src"), P("tgt"), P()),
        out_specs=(P(("src", "tgt"), None), P(), P("tgt")),
        check_vma=False,
    )
```

```python
import functools

import jax
import jax.numpy as jnp
from jax import lax
from jax.experimental import pallas as pl
from jax.experimental.pallas import tpu as pltpu
from jax.sharding import PartitionSpec as P

MESH = pl.DeviceIdType.MESH
D = 384
ROWS = 256
COLS = 768
SLAB = 12
TOTAL = 4096 * 24576

PAIR = (0, 1)


def near_mask(d):
    return (((d >> 2) & 1) << 1, ((d & 3) << 1) | (((d >> 3) & 1) << 3))


def wide_mask(e):
    return (((e & 3) << 2) | ((e >> 3) & 1), ((e >> 2) & 1) << 4)


def place(s, t):
    return (t // 2 % 4, s // 2, (s % 2) * 4 + t // 8)


def ring(a, b, n):
    return min(abs(a - b), n - abs(a - b))


def hops(mask):
    most = 0
    for s in range(16):
        for t in range(32):
            a, b = place(s, t), place(s ^ mask[0], t ^ mask[1])
            most = max(most, ring(a[0], b[0], 4) + ring(a[1], b[1], 8) + ring(a[2], b[2], 8))
    return most


def far_first(masks):
    return sorted(range(1, len(masks)), key=lambda d: -hops(masks[d]))


NEAR = [near_mask(d) for d in range(16)]
WIDE = [wide_mask(d) for d in range(16)]
TGT = [(0, d) for d in range(32)]
SRC = [(d, 0) for d in range(16)]
TILE = [(0, 2 * d) for d in range(16)]
NEAR_ORDER, WIDE_ORDER, TGT_ORDER, SRC_ORDER, TILE_ORDER = map(far_first, (NEAR, WIDE, TGT, SRC, TILE))
GREET = sorted({PAIR, *NEAR[1:], *WIDE[1:], *TGT[1:], *SRC[1:]})


def bits_of(value, n):
    return [lax.rem(lax.div(value, 1 << k), 2) for k in range(n)]


def flipped(value, bits, mask):
    for k, bit in enumerate(bits):
        if (mask >> k) & 1:
            value = value + (1 << k) * (1 - 2 * bit)
    return value


def pieces(x):
    high = x.astype(jnp.bfloat16)
    return high, (x - high.astype(jnp.float32)).astype(jnp.bfloat16)


def dot(a, b, contract=((1,), (0,))):
    def one(left, right):
        return lax.dot_general(left, right, (contract, ((), ())), preferred_element_type=jnp.float32)

    return one(a[0], b[0]) + (one(a[0], b[1]) + one(a[1], b[0]))


def body(
    s_hbm, t_hbm, p_hbm, a_hbm, b_hbm, eps_hbm,
    out_ref, core_ref, col_ref,
    s_ref, t_ref, p_ref, a_ref, b_ref, eps_ref,
    sth, stl, th, tl, half, pair_in, acc, near_in, wide, gathered, kern, adown, row_in, col_in, part, part_in, mine, last_in,
    load, send, recv,
):
    si, ti = lax.axis_index("src"), lax.axis_index("tgt")
    sb, tb = bits_of(si, 4), bits_of(ti, 5)
    core = tb[0]
    g = tb[1] + 2 * tb[2] + 4 * sb[1] + 8 * tb[3]
    gb = [tb[1], tb[2], sb[1], tb[3]]
    w = sb[2] + 2 * sb[3] + 4 * tb[4] + 8 * sb[0]
    tile = tb[1] + 2 * tb[2] + 4 * tb[3] + 8 * tb[4]
    tileb = tb[1:]
    pending = []

    def device(mask):
        return (flipped(si, sb, mask[0]), flipped(ti, tb, mask[1]))

    def copy(src, dst, k, mask):
        return pltpu.make_async_remote_copy(
            src, dst, send.at[k], recv.at[k], device_id=device(mask), device_id_type=MESH
        )

    def arrived(ref, k):
        copy(ref, ref, k, PAIR).wait_recv()
        pending.append((ref, k))

    loads = [
        pltpu.make_async_copy(src, dst, load.at[k])
        for k, (src, dst) in enumerate(
            (
                (s_hbm, s_ref), (t_hbm, t_ref), (p_hbm, p_ref),
                (a_hbm, a_ref), (b_hbm, b_ref), (eps_hbm, eps_ref),
            )
        )
    ]
    for one in loads:
        one.start()
    barrier = pltpu.get_barrier_semaphore()
    for mask in GREET:
        pl.semaphore_signal(barrier, inc=1, device_id=device(mask), device_id_type=MESH)

    def stages():
        loads[0].wait()
        sth[...], stl[...] = pieces(s_ref[...].T)
        loads[1].wait()
        loads[2].wait()
        th[...], tl[...] = pieces(t_ref[...])
        moved = pieces(dot(pieces(p_ref[...]), (th[...], tl[...])))
        for k, h in ((0, 1 - core), (1, core)):
            rows = pl.ds(pl.multiple_of(h * 192, 64), 192)
            value = dot((sth[rows, :], stl[rows, :]), moved)
            for q in range(16):
                half[k, q] = value[q * SLAB : (q + 1) * SLAB]
            if k == 0:
                yield 0
                pl.semaphore_wait(barrier, len(GREET))
                yield 1
                copy(half.at[0], pair_in, 0, PAIR).start()
        for k in (3, 4, 5):
            loads[k].wait()
        mass = a_ref[...].reshape(1, ROWS)
        target = b_ref[...].reshape(1, COLS)
        adown[...] = jnp.broadcast_to(mass, (128, ROWS)).T
        arrived(pair_in, 0)
        acc[...] = half[1] + pair_in[...]
        yield 2

        for d in NEAR_ORDER:
            copy(acc.at[flipped(g, gb, d)], near_in.at[d - 1], 1, NEAR[d]).start()
        arrived(near_in, 1)
        total = acc[g]
        for d in range(15):
            total = total + near_in[d]
        wide[w] = total
        yield 3

        for d in WIDE_ORDER:
            copy(wide.at[w], wide.at[w], 2, WIDE[d]).start()
        arrived(wide.at[pl.ds(0, 15)], 2)
        total = wide[0]
        for d in range(1, 16):
            total = total + wide[d]
        gathered[core, g] = total / TOTAL
        yield 4

        for d in NEAR_ORDER:
            copy(gathered.at[core, g], gathered.at[core, g], 3, NEAR[d]).start()
        arrived(gathered.at[0, pl.ds(0, 15)], 3)
        yield 5
        copy(gathered.at[core], gathered.at[core], 4, PAIR).start()

        def product_of(h):
            rows = pl.ds(pl.multiple_of(h * 192, 64), 192)
            block = jnp.concatenate([gathered[h, q] for q in range(16)], axis=0)
            core_ref[rows, :] = block
            return dot((sth[rows, :], stl[rows, :]), pieces(block), ((0,), (0,)))

        left = product_of(core)
        arrived(gathered.at[0], 4)
        left = (left + product_of(1 - core)) * (2.0 / eps_ref[0])
        yield 6

        kern[...] = p_ref[...] * jnp.exp(dot(pieces(left), (th[...], tl[...]), ((1,), (1,))))
        yield 7

        def settle(x):
            x = x + pltpu.roll(x, 4, 0)
            x = x + pltpu.roll(x, 2, 0)
            return x + pltpu.roll(x, 1, 0)

        def row_total(scale, k, n):
            parts = None
            for j in range(COLS // 128):
                piece = kern[:, j * 128 : (j + 1) * 128]
                if scale is not None:
                    piece = piece * scale[0:1, j * 128 : (j + 1) * 128]
                parts = piece if parts is None else parts + piece
            across = parts.T
            x = across[0:8]
            for j in range(1, 16):
                x = x + across[j * 8 : (j + 1) * 8]
            row_in[n, 0] = settle(x)[0:1]
            for d in TGT_ORDER:
                copy(row_in.at[n, 0], row_in.at[n, d], k, TGT[d]).start()
            arrived(row_in.at[n, pl.ds(0, 31)], k)
            x = row_in[n, 0]
            for d in range(1, 32):
                x = x + row_in[n, d]
            return x

        def col_total(down, k, n):
            pieces = []
            for j in range(COLS // 128):
                piece = kern[:, j * 128 : (j + 1) * 128] * down
                if n == 1:
                    kern[:, j * 128 : (j + 1) * 128] = piece
                x = piece[0:8]
                for i in range(1, 32):
                    x = x + piece[i * 8 : (i + 1) * 8]
                pieces.append(settle(x)[0:1])
            col_in[n, si] = jnp.concatenate(pieces, axis=1)
            for d in SRC_ORDER:
                copy(col_in.at[n, si], col_in.at[n, si], k, SRC[d]).start()
            arrived(col_in.at[n, pl.ds(0, 15)], k)
            x = col_in[n, 0]
            for d in range(1, 16):
                x = x + col_in[n, d]
            return x

        scale = None
        for n in range(2):
            row = mass / row_total(scale, 5 + 2 * n, n)
            yield 8 + 2 * n
            down = jnp.broadcast_to(row, (128, ROWS)).T
            scale = target / col_total(down, 6 + 2 * n, n)
            yield 9 + 2 * n
        col_ref[...] = scale.reshape(COLS)

        kern4 = kern.reshape(16, 2, 8, COLS)
        for k, h in ((0, 1 - core), (1, core)):
            block = kern4[:, h].reshape(128, COLS) * scale
            part[k] = dot(pieces(block), (th[...], tl[...])).reshape(16, 8, D)
            if k == 0:
                copy(part.at[0], part_in, 9, PAIR).start()
        arrived(part_in, 9)
        mine[...] = part[1] + part_in[...]
        yield 12
        for d in TILE_ORDER:
            copy(mine.at[flipped(tile, tileb, d)], last_in.at[d - 1], 10, TILE[d]).start()
        arrived(last_in, 10)
        total = mine[tile]
        for d in range(15):
            total = total + last_in[d]
        own = adown[pl.ds(pl.multiple_of(ti * 8, 8), 8), :]
        for j in range(D // 128):
            out_ref[:, j * 128 : (j + 1) * 128] = total[:, j * 128 : (j + 1) * 128] / own
        yield 13

    for at in stages():
        if at >= STAGE:
            break
    if STAGE < 1:
        pl.semaphore_wait(barrier, len(GREET))
    if STAGE < 2:
        for k in (3, 4, 5):
            loads[k].wait()
    if STAGE == 1:
        pass
    for ref, k in pending:
        copy(ref, ref, k, PAIR).wait_send()


def leave(out_in, core_in, col_in, out_ref, core_ref, col_ref, sem):
    copies = [
        pltpu.make_async_copy(src, dst, sem.at[k])
        for k, (src, dst) in enumerate(((core_in, core_ref), (out_in, out_ref), (col_in, col_ref)))
    ]
    for one in copies:
        one.start()
    for one in copies:
        one.wait()


STAGE = 99


def per_device(*args):
    f32 = jnp.float32
    vmem = pl.BlockSpec(memory_space=pltpu.VMEM)
    hbm = pl.BlockSpec(memory_space=pltpu.HBM)
    results = (
        jax.ShapeDtypeStruct((8, D), f32),
        jax.ShapeDtypeStruct((D, D), f32),
        jax.ShapeDtypeStruct((COLS,), f32),
    )
    out, core, col = pl.pallas_call(
        body,
        out_shape=results,
        in_specs=[hbm] * 6,
        out_specs=(vmem, vmem, vmem),
        scratch_shapes=[
            pltpu.VMEM((ROWS, D), f32),
            pltpu.VMEM((COLS, D), f32),
            pltpu.VMEM((ROWS, COLS), f32),
            pltpu.VMEM((ROWS,), f32),
            pltpu.VMEM((COLS,), f32),
            pltpu.SMEM((1,), f32),
            pltpu.VMEM((D, ROWS), jnp.bfloat16),
            pltpu.VMEM((D, ROWS), jnp.bfloat16),
            pltpu.VMEM((COLS, D), jnp.bfloat16),
            pltpu.VMEM((COLS, D), jnp.bfloat16),
            pltpu.VMEM((2, 16, SLAB, D), f32),
            pltpu.VMEM((16, SLAB, D), f32),
            pltpu.VMEM((16, SLAB, D), f32),
            pltpu.VMEM((15, SLAB, D), f32),
            pltpu.VMEM((16, SLAB, D), f32),
            pltpu.VMEM((2, 16, SLAB, D), f32),
            pltpu.VMEM((ROWS, COLS), f32),
            pltpu.VMEM((ROWS, 128), f32),
            pltpu.VMEM((2, 32, 1, ROWS), f32),
            pltpu.VMEM((2, 16, 1, COLS), f32),
            pltpu.VMEM((2, 16, 8, D), f32),
            pltpu.VMEM((16, 8, D), f32),
            pltpu.VMEM((16, 8, D), f32),
            pltpu.VMEM((15, 8, D), f32),
            pltpu.SemaphoreType.DMA((6,)),
            pltpu.SemaphoreType.DMA((11,)),
            pltpu.SemaphoreType.DMA((11,)),
        ],
        compiler_params=pltpu.CompilerParams(
            collective_id=0, has_side_effects=True, vmem_limit_bytes=60 * 2**20
        ),
    )(*args)
    out, core, col = pl.pallas_call(
        leave,
        out_shape=results,
        in_specs=[vmem] * 3,
        out_specs=(hbm, hbm, hbm),
        scratch_shapes=[pltpu.SemaphoreType.DMA((3,))],
    )(out, core, col)
    return out, core, col


def solution(mesh):
    return jax.shard_map(
        per_device,
        mesh=mesh,
        in_specs=(P("src", None), P("tgt", None), P("src", "tgt"), P("src"), P("tgt"), P()),
        out_specs=(P(("src", "tgt"), None), P(), P("tgt")),
        check_vma=False,
    )
```

```python
import functools

import jax
import jax.numpy as jnp
from jax import lax
from jax.experimental import pallas as pl
from jax.experimental.pallas import tpu as pltpu
from jax.sharding import PartitionSpec as P

MESH = pl.DeviceIdType.MESH
D = 384
ROWS = 256
COLS = 768
SLAB = 36
HALF = 192
TOTAL = 4096 * 24576

PAIR = (0, 1)


def near_mask(d):
    return (((d >> 2) & 1) << 1, ((d & 3) << 1) | (((d >> 3) & 1) << 3))


def wide_mask(e):
    return (((e & 3) << 2) | ((e >> 3) & 1), ((e >> 2) & 1) << 4)


def place(s, t):
    return (t // 2 % 4, s // 2, (s % 2) * 4 + t // 8)


def ring(a, b, n):
    return min(abs(a - b), n - abs(a - b))


def hops(mask):
    most = 0
    for s in range(16):
        for t in range(32):
            a, b = place(s, t), place(s ^ mask[0], t ^ mask[1])
            most = max(most, ring(a[0], b[0], 4) + ring(a[1], b[1], 8) + ring(a[2], b[2], 8))
    return most


def far_first(masks):
    return sorted(range(1, len(masks)), key=lambda d: -hops(masks[d]))


NEAR = [near_mask(d) for d in range(16)]
WIDE = [wide_mask(d) for d in range(16)]
TGT = [(0, d) for d in range(32)]
SRC = [(d, 0) for d in range(16)]
TILE = [(0, 2 * d) for d in range(16)]
NEAR_ORDER, WIDE_ORDER, TGT_ORDER, SRC_ORDER, TILE_ORDER = map(far_first, (NEAR, WIDE, TGT, SRC, TILE))
GREET = sorted({PAIR, *NEAR[1:], *WIDE[1:], *TGT[1:], *SRC[1:]})


def bits_of(value, n):
    return [lax.rem(lax.div(value, 1 << k), 2) for k in range(n)]


def flipped(value, bits, mask):
    for k, bit in enumerate(bits):
        if (mask >> k) & 1:
            value = value + (1 << k) * (1 - 2 * bit)
    return value


def pieces(x):
    high = x.astype(jnp.bfloat16)
    return high, (x - high.astype(jnp.float32)).astype(jnp.bfloat16)


def dot(a, b, contract=((1,), (0,))):
    def one(left, right):
        return lax.dot_general(left, right, (contract, ((), ())), preferred_element_type=jnp.float32)

    return one(a[0], b[0]) + (one(a[0], b[1]) + one(a[1], b[0]))


def body(
    s_hbm, t_hbm, p_hbm, a_hbm, b_hbm, eps_hbm,
    out_ref, core_ref, col_ref,
    s_ref, t_ref, p_ref, a_ref, b_ref, eps_ref,
    sth, stl, th, tl, half, pair_in, acc, near_in, wide, gathered, kern, adown, row_in, col_in, part, part_in, mine, last_in,
    load, send, recv,
):
    si, ti = lax.axis_index("src"), lax.axis_index("tgt")
    sb, tb = bits_of(si, 4), bits_of(ti, 5)
    core = tb[0]
    g = tb[1] + 2 * tb[2] + 4 * sb[1] + 8 * tb[3]
    gb = [tb[1], tb[2], sb[1], tb[3]]
    w = sb[2] + 2 * sb[3] + 4 * tb[4] + 8 * sb[0]
    tile = tb[1] + 2 * tb[2] + 4 * tb[3] + 8 * tb[4]
    tileb = tb[1:]
    pending = []

    def device(mask):
        return (flipped(si, sb, mask[0]), flipped(ti, tb, mask[1]))

    def copy(src, dst, k, mask):
        return pltpu.make_async_remote_copy(
            src, dst, send.at[k], recv.at[k], device_id=device(mask), device_id_type=MESH
        )

    def arrived(ref, k):
        copy(ref, ref, k, PAIR).wait_recv()
        pending.append((ref, k))

    third = COLS // 3
    ranges = []
    for j in range(3):
        some = pl.ds(j * third, third)
        ranges += [(t_hbm.at[some, :], t_ref.at[some, :]), (p_hbm.at[:, some], p_ref.at[:, some])]
    ranges += [(s_hbm, s_ref), (a_hbm, a_ref), (b_hbm, b_ref), (eps_hbm, eps_ref)]
    loads = [pltpu.make_async_copy(src, dst, load.at[k]) for k, (src, dst) in enumerate(ranges)]
    for one in loads:
        one.start()
    barrier = pltpu.get_barrier_semaphore()
    for mask in GREET:
        pl.semaphore_signal(barrier, inc=1, device_id=device(mask), device_id_type=MESH)

    def stages():
        moved = None
        for j in range(3):
            loads[2 * j].wait()
            loads[2 * j + 1].wait()
            some = slice(j * third, (j + 1) * third)
            th[some], tl[some] = pieces(t_ref[some])
            term = dot(pieces(p_ref[:, some]), (th[some], tl[some]))
            moved = term if moved is None else moved + term
        loads[6].wait()
        sth[...], stl[...] = pieces(s_ref[...].T)
        moved = pieces(moved)
        for k, h in ((0, 1 - core), (1, core)):
            rows = pl.ds(pl.multiple_of(h * HALF, 64), HALF)
            value = dot((sth[rows, :], stl[rows, :]), moved)
            flat = jnp.concatenate([value[:, j * 128 : (j + 1) * 128] for j in range(3)], axis=0)
            for q in range(16):
                half[k, q] = flat[q * SLAB : (q + 1) * SLAB]
            if k == 0:
                yield 0
                pl.semaphore_wait(barrier, len(GREET))
                yield 1
                copy(half.at[0], pair_in, 0, PAIR).start()
        for k in (7, 8, 9):
            loads[k].wait()
        mass = a_ref[...].reshape(1, ROWS)
        target = b_ref[...].reshape(1, COLS)
        adown[...] = jnp.broadcast_to(mass, (128, ROWS)).T
        arrived(pair_in, 0)
        acc[...] = half[1] + pair_in[...]
        yield 2

        for d in NEAR_ORDER:
            copy(acc.at[flipped(g, gb, d)], near_in.at[d - 1], 1, NEAR[d]).start()
        arrived(near_in, 1)
        total = acc[g]
        for d in range(15):
            total = total + near_in[d]
        wide[w] = total
        yield 3

        for d in WIDE_ORDER:
            copy(wide.at[w], wide.at[w], 2, WIDE[d]).start()
        arrived(wide.at[pl.ds(0, 15)], 2)
        total = wide[0]
        for d in range(1, 16):
            total = total + wide[d]
        gathered[core, g] = total / TOTAL
        yield 4

        for d in NEAR_ORDER:
            copy(gathered.at[core, g], gathered.at[core, g], 3, NEAR[d]).start()
        arrived(gathered.at[0, pl.ds(0, 15)], 3)
        yield 5
        copy(gathered.at[core], gathered.at[core], 4, PAIR).start()

        def product_of(h):
            rows = pl.ds(pl.multiple_of(h * HALF, 64), HALF)
            flat = jnp.concatenate([gathered[h, q] for q in range(16)], axis=0)
            block = jnp.concatenate([flat[j * HALF : (j + 1) * HALF] for j in range(3)], axis=1)
            core_ref[rows, :] = block
            return dot((sth[rows, :], stl[rows, :]), pieces(block), ((0,), (0,)))

        left = product_of(core)
        arrived(gathered.at[0], 4)
        left = (left + product_of(1 - core)) * (2.0 / eps_ref[0])
        yield 6

        kern[...] = p_ref[...] * jnp.exp(dot(pieces(left), (th[...], tl[...]), ((1,), (1,))))
        yield 7

        def settle(x):
            x = x + pltpu.roll(x, 4, 0)
            x = x + pltpu.roll(x, 2, 0)
            return x + pltpu.roll(x, 1, 0)

        def row_total(scale, k, n):
            parts = None
            for j in range(COLS // 128):
                piece = kern[:, j * 128 : (j + 1) * 128]
                if scale is not None:
                    piece = piece * scale[0:1, j * 128 : (j + 1) * 128]
                parts = piece if parts is None else parts + piece
            across = parts.T
            x = across[0:8]
            for j in range(1, 16):
                x = x + across[j * 8 : (j + 1) * 8]
            row_in[n, 0] = settle(x)[0:1]
            for d in TGT_ORDER:
                copy(row_in.at[n, 0], row_in.at[n, d], k, TGT[d]).start()
            arrived(row_in.at[n, pl.ds(0, 31)], k)
            x = row_in[n, 0]
            for d in range(1, 32):
                x = x + row_in[n, d]
            return x

        def col_total(down, k, n):
            pieces = []
            for j in range(COLS // 128):
                piece = kern[:, j * 128 : (j + 1) * 128] * down
                if n == 1:
                    kern[:, j * 128 : (j + 1) * 128] = piece
                x = piece[0:8]
                for i in range(1, 32):
                    x = x + piece[i * 8 : (i + 1) * 8]
                pieces.append(settle(x)[0:1])
            col_in[n, si] = jnp.concatenate(pieces, axis=1)
            for d in SRC_ORDER:
                copy(col_in.at[n, si], col_in.at[n, si], k, SRC[d]).start()
            arrived(col_in.at[n, pl.ds(0, 15)], k)
            x = col_in[n, 0]
            for d in range(1, 16):
                x = x + col_in[n, d]
            return x

        scale = None
        for n in range(2):
            row = mass / row_total(scale, 5 + 2 * n, n)
            yield 8 + 2 * n
            down = jnp.broadcast_to(row, (128, ROWS)).T
            scale = target / col_total(down, 6 + 2 * n, n)
            yield 9 + 2 * n
        col_ref[...] = scale.reshape(COLS)

        kern4 = kern.reshape(16, 2, 8, COLS)
        for k, h in ((0, 1 - core), (1, core)):
            block = kern4[:, h].reshape(128, COLS) * scale
            part[k] = dot(pieces(block), (th[...], tl[...])).reshape(16, 8, D)
            if k == 0:
                copy(part.at[0], part_in, 9, PAIR).start()
        arrived(part_in, 9)
        mine[...] = part[1] + part_in[...]
        yield 12
        for d in TILE_ORDER:
            copy(mine.at[flipped(tile, tileb, d)], last_in.at[d - 1], 10, TILE[d]).start()
        arrived(last_in, 10)
        total = mine[tile]
        for d in range(15):
            total = total + last_in[d]
        own = adown[pl.ds(pl.multiple_of(ti * 8, 8), 8), :]
        for j in range(D // 128):
            out_ref[:, j * 128 : (j + 1) * 128] = total[:, j * 128 : (j + 1) * 128] / own
        yield 13

    for at in stages():
        if at >= STAGE:
            break
    if STAGE < 1:
        pl.semaphore_wait(barrier, len(GREET))
    if STAGE < 2:
        for k in (7, 8, 9):
            loads[k].wait()
    for ref, k in pending:
        copy(ref, ref, k, PAIR).wait_send()


def leave(out_in, core_in, col_in, out_ref, core_ref, col_ref, sem):
    copies = [
        pltpu.make_async_copy(src, dst, sem.at[k])
        for k, (src, dst) in enumerate(((core_in, core_ref), (out_in, out_ref), (col_in, col_ref)))
    ]
    for one in copies:
        one.start()
    for one in copies:
        one.wait()


STAGE = 99


def per_device(*args):
    f32 = jnp.float32
    vmem = pl.BlockSpec(memory_space=pltpu.VMEM)
    hbm = pl.BlockSpec(memory_space=pltpu.HBM)
    results = (
        jax.ShapeDtypeStruct((8, D), f32),
        jax.ShapeDtypeStruct((D, D), f32),
        jax.ShapeDtypeStruct((COLS,), f32),
    )
    out, core, col = pl.pallas_call(
        body,
        out_shape=results,
        in_specs=[hbm] * 6,
        out_specs=(vmem, vmem, vmem),
        scratch_shapes=[
            pltpu.VMEM((ROWS, D), f32),
            pltpu.VMEM((COLS, D), f32),
            pltpu.VMEM((ROWS, COLS), f32),
            pltpu.VMEM((ROWS,), f32),
            pltpu.VMEM((COLS,), f32),
            pltpu.SMEM((1,), f32),
            pltpu.VMEM((D, ROWS), jnp.bfloat16),
            pltpu.VMEM((D, ROWS), jnp.bfloat16),
            pltpu.VMEM((COLS, D), jnp.bfloat16),
            pltpu.VMEM((COLS, D), jnp.bfloat16),
            pltpu.VMEM((2, 16, SLAB, 128), f32),
            pltpu.VMEM((16, SLAB, 128), f32),
            pltpu.VMEM((16, SLAB, 128), f32),
            pltpu.VMEM((15, SLAB, 128), f32),
            pltpu.VMEM((16, SLAB, 128), f32),
            pltpu.VMEM((2, 16, SLAB, 128), f32),
            pltpu.VMEM((ROWS, COLS), f32),
            pltpu.VMEM((ROWS, 128), f32),
            pltpu.VMEM((2, 32, 1, ROWS), f32),
            pltpu.VMEM((2, 16, 1, COLS), f32),
            pltpu.VMEM((2, 16, 8, D), f32),
            pltpu.VMEM((16, 8, D), f32),
            pltpu.VMEM((16, 8, D), f32),
            pltpu.VMEM((15, 8, D), f32),
            pltpu.SemaphoreType.DMA((10,)),
            pltpu.SemaphoreType.DMA((11,)),
            pltpu.SemaphoreType.DMA((11,)),
        ],
        compiler_params=pltpu.CompilerParams(
            collective_id=0, has_side_effects=True, vmem_limit_bytes=60 * 2**20
        ),
    )(*args)
    out, core, col = pl.pallas_call(
        leave,
        out_shape=results,
        in_specs=[vmem] * 3,
        out_specs=(hbm, hbm, hbm),
        scratch_shapes=[pltpu.SemaphoreType.DMA((3,))],
    )(out, core, col)
    return out, core, col


def solution(mesh):
    return jax.shard_map(
        per_device,
        mesh=mesh,
        in_specs=(P("src", None), P("tgt", None), P("src", "tgt"), P("src"), P("tgt"), P()),
        out_specs=(P(("src", "tgt"), None), P(), P("tgt")),
        check_vma=False,
    )
```

```python
import functools

import jax
import jax.numpy as jnp
from jax import lax
from jax.experimental import pallas as pl
from jax.experimental.pallas import tpu as pltpu
from jax.sharding import PartitionSpec as P

MESH = pl.DeviceIdType.MESH
D = 384
ROWS = 256
COLS = 768
SLAB = 36
HALF = 192
TOTAL = 4096 * 24576

PAIR = (0, 1)


def near_mask(d):
    return (((d >> 2) & 1) << 1, ((d & 3) << 1) | (((d >> 3) & 1) << 3))


def wide_mask(e):
    return (((e & 3) << 2) | ((e >> 3) & 1), ((e >> 2) & 1) << 4)


def place(s, t):
    return (t // 2 % 4, s // 2, (s % 2) * 4 + t // 8)


def ring(a, b, n):
    return min(abs(a - b), n - abs(a - b))


def hops(mask):
    most = 0
    for s in range(16):
        for t in range(32):
            a, b = place(s, t), place(s ^ mask[0], t ^ mask[1])
            most = max(most, ring(a[0], b[0], 4) + ring(a[1], b[1], 8) + ring(a[2], b[2], 8))
    return most


def far_first(masks):
    return sorted(range(1, len(masks)), key=lambda d: -hops(masks[d]))


NEAR = [near_mask(d) for d in range(16)]
WIDE = [wide_mask(d) for d in range(16)]
TGT = [(0, d) for d in range(32)]
SRC = [(d, 0) for d in range(16)]
TILE = [(0, 2 * d) for d in range(16)]
NEAR_ORDER, WIDE_ORDER, TGT_ORDER, SRC_ORDER, TILE_ORDER = map(far_first, (NEAR, WIDE, TGT, SRC, TILE))
EARLY = [d for d in NEAR_ORDER if hops(NEAR[d]) <= 2]
LATE = [d for d in NEAR_ORDER if hops(NEAR[d]) > 2]
GREET = sorted({PAIR, *NEAR[1:], *WIDE[1:]})


def bits_of(value, n):
    return [lax.rem(lax.div(value, 1 << k), 2) for k in range(n)]


def flipped(value, bits, mask):
    for k, bit in enumerate(bits):
        if (mask >> k) & 1:
            value = value + (1 << k) * (1 - 2 * bit)
    return value


def pieces(x):
    high = x.astype(jnp.bfloat16)
    return high, (x - high.astype(jnp.float32)).astype(jnp.bfloat16)


def dot(a, b, contract=((1,), (0,))):
    def one(left, right):
        return lax.dot_general(left, right, (contract, ((), ())), preferred_element_type=jnp.float32)

    return one(a[0], b[0]) + (one(a[0], b[1]) + one(a[1], b[0]))


def body(
    s_hbm, t_hbm, p_hbm, a_hbm, b_hbm, eps_hbm,
    out_ref, core_hbm, col_hbm,
    core_ref, col_ref, s_ref, t_ref, p_ref, a_ref, b_ref, eps_ref,
    sth, stl, th, tl, half, pair_in, acc, near_in, wide, gathered, kern, adown, row_in, col_in, part, part_in, mine, last_in,
    load, send, recv,
):
    si, ti = lax.axis_index("src"), lax.axis_index("tgt")
    sb, tb = bits_of(si, 4), bits_of(ti, 5)
    core = tb[0]
    g = tb[1] + 2 * tb[2] + 4 * sb[1] + 8 * tb[3]
    gb = [tb[1], tb[2], sb[1], tb[3]]
    w = sb[2] + 2 * sb[3] + 4 * tb[4] + 8 * sb[0]
    tile = tb[1] + 2 * tb[2] + 4 * tb[3] + 8 * tb[4]
    tileb = tb[1:]
    pending = []

    def device(mask):
        return (flipped(si, sb, mask[0]), flipped(ti, tb, mask[1]))

    def copy(src, dst, k, mask):
        return pltpu.make_async_remote_copy(
            src, dst, send.at[k], recv.at[k], device_id=device(mask), device_id_type=MESH
        )

    def arrived(ref, k):
        copy(ref, ref, k, PAIR).wait_recv()
        pending.append((ref, k))

    third = COLS // 3
    ranges = []
    for j in range(3):
        some = pl.ds(j * third, third)
        ranges += [(t_hbm.at[some, :], t_ref.at[some, :]), (p_hbm.at[:, some], p_ref.at[:, some])]
    ranges += [(s_hbm, s_ref), (a_hbm, a_ref), (b_hbm, b_ref), (eps_hbm, eps_ref)]
    loads = [pltpu.make_async_copy(src, dst, load.at[k]) for k, (src, dst) in enumerate(ranges)]
    for one in loads:
        one.start()
    barrier = pltpu.get_barrier_semaphore()
    for mask in GREET:
        pl.semaphore_signal(barrier, inc=1, device_id=device(mask), device_id_type=MESH)

    moved = None
    for j in range(3):
        loads[2 * j].wait()
        loads[2 * j + 1].wait()
        some = slice(j * third, (j + 1) * third)
        th[some], tl[some] = pieces(t_ref[some])
        term = dot(pieces(p_ref[:, some]), (th[some], tl[some]))
        moved = term if moved is None else moved + term
    loads[6].wait()
    sth[...], stl[...] = pieces(s_ref[...].T)
    moved = pieces(moved)
    for k, h in ((0, 1 - core), (1, core)):
        rows = pl.ds(pl.multiple_of(h * HALF, 64), HALF)
        value = dot((sth[rows, :], stl[rows, :]), moved)
        flat = jnp.concatenate([value[:, j * 128 : (j + 1) * 128] for j in range(3)], axis=0)
        for q in range(16):
            half[k, q] = flat[q * SLAB : (q + 1) * SLAB]
        if k == 0:
            pl.semaphore_wait(barrier, len(GREET))
            copy(half.at[0], pair_in, 0, PAIR).start()
    for k in (7, 8, 9):
        loads[k].wait()
    mass = a_ref[...].reshape(1, ROWS)
    target = b_ref[...].reshape(1, COLS)
    adown[...] = jnp.broadcast_to(mass, (128, ROWS)).T
    arrived(pair_in, 0)
    acc[...] = half[1] + pair_in[...]

    for d in NEAR_ORDER:
        copy(acc.at[flipped(g, gb, d)], near_in.at[d - 1], 1, NEAR[d]).start()
    arrived(near_in, 1)
    total = acc[g]
    for d in range(15):
        total = total + near_in[d]
    wide[w] = total

    for d in WIDE_ORDER:
        copy(wide.at[w], wide.at[w], 2, WIDE[d]).start()
    arrived(wide.at[pl.ds(0, 15)], 2)
    total = wide[0]
    for d in range(1, 16):
        total = total + wide[d]
    gathered[core, g] = total / TOTAL

    for d in LATE:
        copy(gathered.at[core, g], gathered.at[core, g], 11, NEAR[d]).start()
    for d in EARLY:
        copy(gathered.at[core, g], gathered.at[core, g], 3, NEAR[d]).start()
    copy(gathered.at[core, g], gathered.at[core, g], 4, PAIR).start()
    for group, k in ((EARLY, 3), (LATE, 11)):
        arrived(gathered.at[0, pl.ds(0, len(group))], k)
        for d in group:
            slab = gathered.at[core, flipped(g, gb, d)]
            copy(slab, slab, 4, PAIR).start()

    def product_of(h):
        rows = pl.ds(pl.multiple_of(h * HALF, 64), HALF)
        flat = jnp.concatenate([gathered[h, q] for q in range(16)], axis=0)
        block = jnp.concatenate([flat[j * HALF : (j + 1) * HALF] for j in range(3)], axis=1)
        core_ref[rows, :] = block
        return dot((sth[rows, :], stl[rows, :]), pieces(block), ((0,), (0,)))

    left = product_of(core)
    arrived(gathered.at[0], 4)
    left = (left + product_of(1 - core)) * (2.0 / eps_ref[0])

    leaving = [
        pltpu.make_async_copy(core_ref, core_hbm, load.at[10]),
        pltpu.make_async_copy(col_ref, col_hbm, load.at[11]),
    ]
    leaving[0].start()

    kern[...] = p_ref[...] * jnp.exp(dot(pieces(left), (th[...], tl[...]), ((1,), (1,))))

    def settle(x):
        x = x + pltpu.roll(x, 4, 0)
        x = x + pltpu.roll(x, 2, 0)
        return x + pltpu.roll(x, 1, 0)

    def row_total(scale, k, n):
        parts = None
        for j in range(COLS // 128):
            piece = kern[:, j * 128 : (j + 1) * 128]
            if scale is not None:
                piece = piece * scale[0:1, j * 128 : (j + 1) * 128]
            parts = piece if parts is None else parts + piece
        across = parts.T
        x = across[0:8]
        for j in range(1, 16):
            x = x + across[j * 8 : (j + 1) * 8]
        row_in[n, 0] = settle(x)[0:1]
        for d in TGT_ORDER:
            copy(row_in.at[n, 0], row_in.at[n, d], k, TGT[d]).start()
        arrived(row_in.at[n, pl.ds(0, 31)], k)
        x = row_in[n, 0]
        for d in range(1, 32):
            x = x + row_in[n, d]
        return x

    def col_total(down, k, n):
        pieces = []
        for j in range(COLS // 128):
            piece = kern[:, j * 128 : (j + 1) * 128] * down
            if n == 1:
                kern[:, j * 128 : (j + 1) * 128] = piece
            x = piece[0:8]
            for i in range(1, 32):
                x = x + piece[i * 8 : (i + 1) * 8]
            pieces.append(settle(x)[0:1])
        col_in[n, si] = jnp.concatenate(pieces, axis=1)
        for d in SRC_ORDER:
            copy(col_in.at[n, si], col_in.at[n, si], k, SRC[d]).start()
        arrived(col_in.at[n, pl.ds(0, 15)], k)
        x = col_in[n, 0]
        for d in range(1, 16):
            x = x + col_in[n, d]
        return x

    scale = None
    for n in range(2):
        row = mass / row_total(scale, 5 + 2 * n, n)
        down = jnp.broadcast_to(row, (128, ROWS)).T
        scale = target / col_total(down, 6 + 2 * n, n)
    col_ref[...] = scale.reshape(COLS)
    leaving[1].start()

    kern4 = kern.reshape(16, 2, 8, COLS)
    for k, h in ((0, 1 - core), (1, core)):
        block = kern4[:, h].reshape(128, COLS) * scale
        part[k] = dot(pieces(block), (th[...], tl[...])).reshape(16, 8, D)
        if k == 0:
            copy(part.at[0], part_in, 9, PAIR).start()
    arrived(part_in, 9)
    mine[...] = part[1] + part_in[...]
    for d in TILE_ORDER:
        copy(mine.at[flipped(tile, tileb, d)], last_in.at[d - 1], 10, TILE[d]).start()
    arrived(last_in, 10)
    total = mine[tile]
    for d in range(15):
        total = total + last_in[d]
    own = adown[pl.ds(pl.multiple_of(ti * 8, 8), 8), :]
    for j in range(D // 128):
        out_ref[:, j * 128 : (j + 1) * 128] = total[:, j * 128 : (j + 1) * 128] / own

    for one in leaving:
        one.wait()
    for ref, k in pending:
        copy(ref, ref, k, PAIR).wait_send()


def leave(out_in, core_in, col_in, out_ref, core_ref, col_ref, sem):
    pairs = [(out_in, out_ref), (col_in, col_ref)]
    for j in range(4):
        rows = pl.ds(j * (D // 4), D // 4)
        pairs.append((core_in.at[rows], core_ref.at[rows]))
    copies = [pltpu.make_async_copy(src, dst, sem.at[k]) for k, (src, dst) in enumerate(pairs)]
    for one in copies:
        one.start()
    for one in copies:
        one.wait()


def per_device(*args):
    f32 = jnp.float32
    vmem = pl.BlockSpec(memory_space=pltpu.VMEM)
    hbm = pl.BlockSpec(memory_space=pltpu.HBM)
    results = (
        jax.ShapeDtypeStruct((8, D), f32),
        jax.ShapeDtypeStruct((D, D), f32),
        jax.ShapeDtypeStruct((COLS,), f32),
    )
    out, core, col = pl.pallas_call(
        body,
        out_shape=results,
        in_specs=[hbm] * 6,
        out_specs=(vmem, hbm, hbm),
        scratch_shapes=[
            pltpu.VMEM((D, D), f32),
            pltpu.VMEM((COLS,), f32),
            pltpu.VMEM((ROWS, D), f32),
            pltpu.VMEM((COLS, D), f32),
            pltpu.VMEM((ROWS, COLS), f32),
            pltpu.VMEM((ROWS,), f32),
            pltpu.VMEM((COLS,), f32),
            pltpu.SMEM((1,), f32),
            pltpu.VMEM((D, ROWS), jnp.bfloat16),
            pltpu.VMEM((D, ROWS), jnp.bfloat16),
            pltpu.VMEM((COLS, D), jnp.bfloat16),
            pltpu.VMEM((COLS, D), jnp.bfloat16),
            pltpu.VMEM((2, 16, SLAB, 128), f32),
            pltpu.VMEM((16, SLAB, 128), f32),
            pltpu.VMEM((16, SLAB, 128), f32),
            pltpu.VMEM((15, SLAB, 128), f32),
            pltpu.VMEM((16, SLAB, 128), f32),
            pltpu.VMEM((2, 16, SLAB, 128), f32),
            pltpu.VMEM((ROWS, COLS), f32),
            pltpu.VMEM((ROWS, 128), f32),
            pltpu.VMEM((2, 32, 1, ROWS), f32),
            pltpu.VMEM((2, 16, 1, COLS), f32),
            pltpu.VMEM((2, 16, 8, D), f32),
            pltpu.VMEM((16, 8, D), f32),
            pltpu.VMEM((16, 8, D), f32),
            pltpu.VMEM((15, 8, D), f32),
            pltpu.SemaphoreType.DMA((12,)),
            pltpu.SemaphoreType.DMA((12,)),
            pltpu.SemaphoreType.DMA((12,)),
        ],
        compiler_params=pltpu.CompilerParams(
            collective_id=0, has_side_effects=True, vmem_limit_bytes=60 * 2**20
        ),
    )(*args)
    out, core, col = pl.pallas_call(
        leave,
        out_shape=results,
        in_specs=[hbm] * 3,
        out_specs=(hbm, hbm, hbm),
        scratch_shapes=[pltpu.SemaphoreType.DMA((6,))],
        compiler_params=pltpu.CompilerParams(vmem_limit_bytes=60 * 2**20),
    )(out, core, col)
    return out, core, col


def solution(mesh):
    return jax.shard_map(
        per_device,
        mesh=mesh,
        in_specs=(P("src", None), P("tgt", None), P("src", "tgt"), P("src"), P("tgt"), P()),
        out_specs=(P(("src", "tgt"), None), P(), P("tgt")),
        check_vma=False,
    )
```

```python
import functools

import jax
import jax.numpy as jnp
from jax import lax
from jax.experimental import pallas as pl
from jax.experimental.pallas import tpu as pltpu
from jax.sharding import PartitionSpec as P

MESH = pl.DeviceIdType.MESH
D = 384
ROWS = 256
COLS = 768
SLAB = 36
HALF = 192
TOTAL = 4096 * 24576

PAIR = (0, 1)


def near_mask(d):
    return (((d >> 2) & 1) << 1, ((d & 3) << 1) | (((d >> 3) & 1) << 3))


def wide_mask(e):
    return (((e & 3) << 2) | ((e >> 3) & 1), ((e >> 2) & 1) << 4)


def place(s, t):
    return (t // 2 % 4, s // 2, (s % 2) * 4 + t // 8)


def ring(a, b, n):
    return min(abs(a - b), n - abs(a - b))


def hops(mask):
    most = 0
    for s in range(16):
        for t in range(32):
            a, b = place(s, t), place(s ^ mask[0], t ^ mask[1])
            most = max(most, ring(a[0], b[0], 4) + ring(a[1], b[1], 8) + ring(a[2], b[2], 8))
    return most


def far_first(masks):
    return sorted(range(1, len(masks)), key=lambda d: -hops(masks[d]))


NEAR = [near_mask(d) for d in range(16)]
WIDE = [wide_mask(d) for d in range(16)]
TGT = [(0, d) for d in range(32)]
SRC = [(d, 0) for d in range(16)]
TILE = [(0, 2 * d) for d in range(16)]
NEAR_ORDER, WIDE_ORDER, TGT_ORDER, SRC_ORDER, TILE_ORDER = map(far_first, (NEAR, WIDE, TGT, SRC, TILE))
EARLY = [d for d in NEAR_ORDER if hops(NEAR[d]) <= 2]
LATE = [d for d in NEAR_ORDER if hops(NEAR[d]) > 2]
GREET = sorted({PAIR, *NEAR[1:], *WIDE[1:]})


def bits_of(value, n):
    return [lax.rem(lax.div(value, 1 << k), 2) for k in range(n)]


def flipped(value, bits, mask):
    for k, bit in enumerate(bits):
        if (mask >> k) & 1:
            value = value + (1 << k) * (1 - 2 * bit)
    return value


def pieces(x):
    high = x.astype(jnp.bfloat16)
    return high, (x - high.astype(jnp.float32)).astype(jnp.bfloat16)


def dot(a, b, contract=((1,), (0,))):
    def one(left, right):
        return lax.dot_general(left, right, (contract, ((), ())), preferred_element_type=jnp.float32)

    return one(a[0], b[0]) + (one(a[0], b[1]) + one(a[1], b[0]))


def body(
    s_hbm, t_hbm, p_hbm, a_hbm, b_hbm, eps_hbm,
    out_ref, core_ref, col_ref,
    s_ref, t_ref, p_ref, a_ref, b_ref, eps_ref,
    sth, stl, th, tl, half, pair_in, acc, near_in, wide, gathered, kern, adown, row_in, col_in, part, part_in, mine, last_in,
    load, send, recv,
):
    si, ti = lax.axis_index("src"), lax.axis_index("tgt")
    sb, tb = bits_of(si, 4), bits_of(ti, 5)
    core = tb[0]
    g = tb[1] + 2 * tb[2] + 4 * sb[1] + 8 * tb[3]
    gb = [tb[1], tb[2], sb[1], tb[3]]
    w = sb[2] + 2 * sb[3] + 4 * tb[4] + 8 * sb[0]
    tile = tb[1] + 2 * tb[2] + 4 * tb[3] + 8 * tb[4]
    tileb = tb[1:]
    pending = []

    def device(mask):
        return (flipped(si, sb, mask[0]), flipped(ti, tb, mask[1]))

    def copy(src, dst, k, mask):
        return pltpu.make_async_remote_copy(
            src, dst, send.at[k], recv.at[k], device_id=device(mask), device_id_type=MESH
        )

    def arrived(ref, k):
        copy(ref, ref, k, PAIR).wait_recv()
        pending.append((ref, k))

    third = COLS // 3
    ranges = []
    for j in range(3):
        some = pl.ds(j * third, third)
        ranges += [(t_hbm.at[some, :], t_ref.at[some, :]), (p_hbm.at[:, some], p_ref.at[:, some])]
    ranges += [(s_hbm, s_ref), (a_hbm, a_ref), (b_hbm, b_ref), (eps_hbm, eps_ref)]
    loads = [pltpu.make_async_copy(src, dst, load.at[k]) for k, (src, dst) in enumerate(ranges)]
    for one in loads:
        one.start()
    barrier = pltpu.get_barrier_semaphore()
    for mask in GREET:
        pl.semaphore_signal(barrier, inc=1, device_id=device(mask), device_id_type=MESH)

    moved = None
    for j in range(3):
        loads[2 * j].wait()
        loads[2 * j + 1].wait()
        some = slice(j * third, (j + 1) * third)
        th[some], tl[some] = pieces(t_ref[some])
        term = dot(pieces(p_ref[:, some]), (th[some], tl[some]))
        moved = term if moved is None else moved + term
    loads[6].wait()
    sth[...], stl[...] = pieces(s_ref[...].T)
    moved = pieces(moved)
    for k, h in ((0, 1 - core), (1, core)):
        rows = pl.ds(pl.multiple_of(h * HALF, 64), HALF)
        value = dot((sth[rows, :], stl[rows, :]), moved)
        flat = jnp.concatenate([value[:, j * 128 : (j + 1) * 128] for j in range(3)], axis=0)
        for q in range(16):
            half[k, q] = flat[q * SLAB : (q + 1) * SLAB]
        if k == 0:
            pl.semaphore_wait(barrier, len(GREET))
            copy(half.at[0], pair_in, 0, PAIR).start()
    for k in (7, 8, 9):
        loads[k].wait()
    mass = a_ref[...].reshape(1, ROWS)
    target = b_ref[...].reshape(1, COLS)
    adown[...] = jnp.broadcast_to(mass, (128, ROWS)).T
    arrived(pair_in, 0)
    acc[...] = half[1] + pair_in[...]

    for d in NEAR_ORDER:
        copy(acc.at[flipped(g, gb, d)], near_in.at[d - 1], 1, NEAR[d]).start()
    arrived(near_in, 1)
    total = acc[g]
    for d in range(15):
        total = total + near_in[d]
    wide[w] = total

    for d in WIDE_ORDER:
        copy(wide.at[w], wide.at[w], 2, WIDE[d]).start()
    arrived(wide.at[pl.ds(0, 15)], 2)
    total = wide[0]
    for d in range(1, 16):
        total = total + wide[d]
    gathered[core, g] = total / TOTAL

    for d in LATE:
        copy(gathered.at[core, g], gathered.at[core, g], 11, NEAR[d]).start()
    for d in EARLY:
        copy(gathered.at[core, g], gathered.at[core, g], 3, NEAR[d]).start()
    copy(gathered.at[core, g], gathered.at[core, g], 4, PAIR).start()
    for group, k in ((EARLY, 3), (LATE, 11)):
        arrived(gathered.at[0, pl.ds(0, len(group))], k)
        for d in group:
            slab = gathered.at[core, flipped(g, gb, d)]
            copy(slab, slab, 4, PAIR).start()

    def product_of(h):
        rows = pl.ds(pl.multiple_of(h * HALF, 64), HALF)
        flat = jnp.concatenate([gathered[h, q] for q in range(16)], axis=0)
        block = jnp.concatenate([flat[j * HALF : (j + 1) * HALF] for j in range(3)], axis=1)
        core_ref[rows, :] = block
        return dot((sth[rows, :], stl[rows, :]), pieces(block), ((0,), (0,)))

    left = product_of(core)
    arrived(gathered.at[0], 4)
    left = (left + product_of(1 - core)) * (2.0 / eps_ref[0])

    kern[...] = p_ref[...] * jnp.exp(dot(pieces(left), (th[...], tl[...]), ((1,), (1,))))

    def settle(x):
        x = x + pltpu.roll(x, 4, 0)
        x = x + pltpu.roll(x, 2, 0)
        return x + pltpu.roll(x, 1, 0)

    def row_total(scale, k, n):
        parts = None
        for j in range(COLS // 128):
            piece = kern[:, j * 128 : (j + 1) * 128]
            if scale is not None:
                piece = piece * scale[0:1, j * 128 : (j + 1) * 128]
            parts = piece if parts is None else parts + piece
        across = parts.T
        x = across[0:8]
        for j in range(1, 16):
            x = x + across[j * 8 : (j + 1) * 8]
        row_in[n, 0] = settle(x)[0:1]
        for d in TGT_ORDER:
            copy(row_in.at[n, 0], row_in.at[n, d], k, TGT[d]).start()
        arrived(row_in.at[n, pl.ds(0, 31)], k)
        x = row_in[n, 0]
        for d in range(1, 32):
            x = x + row_in[n, d]
        return x

    def col_total(down, k, n):
        pieces = []
        for j in range(COLS // 128):
            piece = kern[:, j * 128 : (j + 1) * 128] * down
            if n == 1:
                kern[:, j * 128 : (j + 1) * 128] = piece
            x = piece[0:8]
            for i in range(1, 32):
                x = x + piece[i * 8 : (i + 1) * 8]
            pieces.append(settle(x)[0:1])
        col_in[n, si] = jnp.concatenate(pieces, axis=1)
        for d in SRC_ORDER:
            copy(col_in.at[n, si], col_in.at[n, si], k, SRC[d]).start()
        arrived(col_in.at[n, pl.ds(0, 15)], k)
        x = col_in[n, 0]
        for d in range(1, 16):
            x = x + col_in[n, d]
        return x

    scale = None
    for n in range(2):
        row = mass / row_total(scale, 5 + 2 * n, n)
        down = jnp.broadcast_to(row, (128, ROWS)).T
        scale = target / col_total(down, 6 + 2 * n, n)
    col_ref[...] = scale.reshape(COLS)

    kern4 = kern.reshape(16, 2, 8, COLS)
    for k, h in ((0, 1 - core), (1, core)):
        block = kern4[:, h].reshape(128, COLS) * scale
        part[k] = dot(pieces(block), (th[...], tl[...])).reshape(16, 8, D)
        if k == 0:
            copy(part.at[0], part_in, 9, PAIR).start()
    arrived(part_in, 9)
    mine[...] = part[1] + part_in[...]
    for d in TILE_ORDER:
        copy(mine.at[flipped(tile, tileb, d)], last_in.at[d - 1], 10, TILE[d]).start()
    arrived(last_in, 10)
    total = mine[tile]
    for d in range(15):
        total = total + last_in[d]
    own = adown[pl.ds(pl.multiple_of(ti * 8, 8), 8), :]
    for j in range(D // 128):
        out_ref[:, j * 128 : (j + 1) * 128] = total[:, j * 128 : (j + 1) * 128] / own

    for ref, k in pending:
        copy(ref, ref, k, PAIR).wait_send()


def leave(out_in, core_in, col_in, out_ref, core_ref, col_ref, sem):
    pairs = ((core_in, core_ref), (out_in, out_ref), (col_in, col_ref))
    copies = [pltpu.make_async_copy(src, dst, sem.at[k]) for k, (src, dst) in enumerate(pairs)]
    for one in copies:
        one.start()
    for one in copies:
        one.wait()


def per_device(*args):
    f32 = jnp.float32
    vmem = pl.BlockSpec(memory_space=pltpu.VMEM)
    hbm = pl.BlockSpec(memory_space=pltpu.HBM)
    results = (
        jax.ShapeDtypeStruct((8, D), f32),
        jax.ShapeDtypeStruct((D, D), f32),
        jax.ShapeDtypeStruct((COLS,), f32),
    )
    out, core, col = pl.pallas_call(
        body,
        out_shape=results,
        in_specs=[hbm] * 6,
        out_specs=(vmem, vmem, vmem),
        scratch_shapes=[
            pltpu.VMEM((ROWS, D), f32),
            pltpu.VMEM((COLS, D), f32),
            pltpu.VMEM((ROWS, COLS), f32),
            pltpu.VMEM((ROWS,), f32),
            pltpu.VMEM((COLS,), f32),
            pltpu.SMEM((1,), f32),
            pltpu.VMEM((D, ROWS), jnp.bfloat16),
            pltpu.VMEM((D, ROWS), jnp.bfloat16),
            pltpu.VMEM((COLS, D), jnp.bfloat16),
            pltpu.VMEM((COLS, D), jnp.bfloat16),
            pltpu.VMEM((2, 16, SLAB, 128), f32),
            pltpu.VMEM((16, SLAB, 128), f32),
            pltpu.VMEM((16, SLAB, 128), f32),
            pltpu.VMEM((15, SLAB, 128), f32),
            pltpu.VMEM((16, SLAB, 128), f32),
            pltpu.VMEM((2, 16, SLAB, 128), f32),
            pltpu.VMEM((ROWS, COLS), f32),
            pltpu.VMEM((ROWS, 128), f32),
            pltpu.VMEM((2, 32, 1, ROWS), f32),
            pltpu.VMEM((2, 16, 1, COLS), f32),
            pltpu.VMEM((2, 16, 8, D), f32),
            pltpu.VMEM((16, 8, D), f32),
            pltpu.VMEM((16, 8, D), f32),
            pltpu.VMEM((15, 8, D), f32),
            pltpu.SemaphoreType.DMA((10,)),
            pltpu.SemaphoreType.DMA((12,)),
            pltpu.SemaphoreType.DMA((12,)),
        ],
        compiler_params=pltpu.CompilerParams(
            collective_id=0, has_side_effects=True, vmem_limit_bytes=40 * 2**20
        ),
    )(*[pltpu.with_memory_space_constraint(x, pltpu.HBM) for x in args[:5]], args[5])
    out, core, col = pl.pallas_call(
        leave,
        out_shape=results,
        in_specs=[vmem] * 3,
        out_specs=(hbm, hbm, hbm),
        scratch_shapes=[pltpu.SemaphoreType.DMA((3,))],
        compiler_params=pltpu.CompilerParams(vmem_limit_bytes=2**20),
    )(out, core, col)
    return out, core, col


def solution(mesh):
    return jax.shard_map(
        per_device,
        mesh=mesh,
        in_specs=(P("src", None), P("tgt", None), P("src", "tgt"), P("src"), P("tgt"), P()),
        out_specs=(P(("src", "tgt"), None), P(), P("tgt")),
        check_vma=False,
    )
```

```python
import functools

import jax
import jax.numpy as jnp
from jax import lax
from jax.experimental import pallas as pl
from jax.experimental.pallas import tpu as pltpu
from jax.sharding import PartitionSpec as P

MESH = pl.DeviceIdType.MESH
D = 384
ROWS = 256
COLS = 768
SLAB = 36
HALF = 192
TOTAL = 4096 * 24576

PAIR = (0, 1)


def near_mask(d):
    return (((d >> 2) & 1) << 1, ((d & 3) << 1) | (((d >> 3) & 1) << 3))


def wide_mask(e):
    return (((e & 3) << 2) | ((e >> 3) & 1), ((e >> 2) & 1) << 4)


def place(s, t):
    return (t // 2 % 4, s // 2, (s % 2) * 4 + t // 8)


def ring(a, b, n):
    return min(abs(a - b), n - abs(a - b))


def hops(mask):
    most = 0
    for s in range(16):
        for t in range(32):
            a, b = place(s, t), place(s ^ mask[0], t ^ mask[1])
            most = max(most, ring(a[0], b[0], 4) + ring(a[1], b[1], 8) + ring(a[2], b[2], 8))
    return most


def far_first(masks):
    return sorted(range(1, len(masks)), key=lambda d: -hops(masks[d]))


NEAR = [near_mask(d) for d in range(16)]
WIDE = [wide_mask(d) for d in range(16)]
TGT = [(0, d) for d in range(32)]
SRC = [(d, 0) for d in range(16)]
TILE = [(0, 2 * d) for d in range(16)]
NEAR_ORDER, WIDE_ORDER, TGT_ORDER, SRC_ORDER, TILE_ORDER = map(far_first, (NEAR, WIDE, TGT, SRC, TILE))
EARLY = [d for d in NEAR_ORDER if hops(NEAR[d]) <= 2]
LATE = [d for d in NEAR_ORDER if hops(NEAR[d]) > 2]
GREET = sorted({PAIR, *NEAR[1:], *WIDE[1:]})


def bits_of(value, n):
    return [lax.rem(lax.div(value, 1 << k), 2) for k in range(n)]


def flipped(value, bits, mask):
    for k, bit in enumerate(bits):
        if (mask >> k) & 1:
            value = value + (1 << k) * (1 - 2 * bit)
    return value


def pieces(x):
    high = x.astype(jnp.bfloat16)
    return high, (x - high.astype(jnp.float32)).astype(jnp.bfloat16)


def dot(a, b, contract=((1,), (0,))):
    def one(left, right):
        return lax.dot_general(left, right, (contract, ((), ())), preferred_element_type=jnp.float32)

    return one(a[0], b[0]) + (one(a[0], b[1]) + one(a[1], b[0]))


def body(
    s_hbm, t_hbm, p_hbm, a_hbm, b_hbm, eps_hbm,
    out_ref, core_ref, col_ref,
    s_ref, t_ref, p_ref, a_ref, b_ref, eps_ref,
    sth, stl, th, tl, half, pair_in, acc, near_in, wide, gathered, kern, adown, row_in, col_in, part, part_in, mine, last_in,
    load, send, recv,
):
    si, ti = lax.axis_index("src"), lax.axis_index("tgt")
    sb, tb = bits_of(si, 4), bits_of(ti, 5)
    core = tb[0]
    g = tb[1] + 2 * tb[2] + 4 * sb[1] + 8 * tb[3]
    gb = [tb[1], tb[2], sb[1], tb[3]]
    w = sb[2] + 2 * sb[3] + 4 * tb[4] + 8 * sb[0]
    tile = tb[1] + 2 * tb[2] + 4 * tb[3] + 8 * tb[4]
    tileb = tb[1:]
    pending = []

    def device(mask):
        return (flipped(si, sb, mask[0]), flipped(ti, tb, mask[1]))

    def copy(src, dst, k, mask):
        return pltpu.make_async_remote_copy(
            src, dst, send.at[k], recv.at[k], device_id=device(mask), device_id_type=MESH
        )

    def arrived(ref, k):
        copy(ref, ref, k, PAIR).wait_recv()
        pending.append((ref, k))

    third = COLS // 3
    ranges = [(s_hbm, s_ref)]
    for j in range(3):
        some = pl.ds(j * third, third)
        ranges += [(t_hbm.at[some, :], t_ref.at[some, :]), (p_hbm.at[:, some], p_ref.at[:, some])]
    ranges += [(a_hbm, a_ref), (b_hbm, b_ref), (eps_hbm, eps_ref)]
    loads = [pltpu.make_async_copy(src, dst, load.at[k]) for k, (src, dst) in enumerate(ranges)]
    for one in loads:
        one.start()
    barrier = pltpu.get_barrier_semaphore()
    for mask in GREET:
        pl.semaphore_signal(barrier, inc=1, device_id=device(mask), device_id_type=MESH)

    loads[0].wait()
    sth[...], stl[...] = pieces(s_ref[...].T)
    moved = None
    for j in range(3):
        loads[2 * j + 1].wait()
        loads[2 * j + 2].wait()
        some = slice(j * third, (j + 1) * third)
        th[some], tl[some] = pieces(t_ref[some])
        term = dot(pieces(p_ref[:, some]), (th[some], tl[some]))
        moved = term if moved is None else moved + term
    moved = pieces(moved)
    for k, h in ((0, 1 - core), (1, core)):
        rows = pl.ds(pl.multiple_of(h * HALF, 64), HALF)
        value = dot((sth[rows, :], stl[rows, :]), moved)
        flat = jnp.concatenate([value[:, j * 128 : (j + 1) * 128] for j in range(3)], axis=0)
        for q in range(16):
            half[k, q] = flat[q * SLAB : (q + 1) * SLAB]
        if k == 0:
            pl.semaphore_wait(barrier, len(GREET))
            copy(half.at[0], pair_in, 0, PAIR).start()
    for k in (7, 8, 9):
        loads[k].wait()
    mass = a_ref[...].reshape(1, ROWS)
    target = b_ref[...].reshape(1, COLS)
    adown[...] = jnp.broadcast_to(mass, (128, ROWS)).T
    arrived(pair_in, 0)
    acc[...] = half[1] + pair_in[...]

    for d in NEAR_ORDER:
        copy(acc.at[flipped(g, gb, d)], near_in.at[d - 1], 1, NEAR[d]).start()
    arrived(near_in, 1)
    total = acc[g]
    for d in range(15):
        total = total + near_in[d]
    wide[w] = total

    for d in WIDE_ORDER:
        copy(wide.at[w], wide.at[w], 2, WIDE[d]).start()
    arrived(wide.at[pl.ds(0, 15)], 2)
    total = wide[0]
    for d in range(1, 16):
        total = total + wide[d]
    gathered[core, g] = total / TOTAL

    for d in LATE:
        copy(gathered.at[core, g], gathered.at[core, g], 11, NEAR[d]).start()
    for d in EARLY:
        copy(gathered.at[core, g], gathered.at[core, g], 3, NEAR[d]).start()
    copy(gathered.at[core, g], gathered.at[core, g], 4, PAIR).start()
    for group, k in ((EARLY, 3), (LATE, 11)):
        arrived(gathered.at[0, pl.ds(0, len(group))], k)
        for d in group:
            slab = gathered.at[core, flipped(g, gb, d)]
            copy(slab, slab, 4, PAIR).start()

    def product_of(h):
        rows = pl.ds(pl.multiple_of(h * HALF, 64), HALF)
        flat = jnp.concatenate([gathered[h, q] for q in range(16)], axis=0)
        block = jnp.concatenate([flat[j * HALF : (j + 1) * HALF] for j in range(3)], axis=1)
        core_ref[rows, :] = block
        return dot((sth[rows, :], stl[rows, :]), pieces(block), ((0,), (0,)))

    left = product_of(core)
    arrived(gathered.at[0], 4)
    left = (left + product_of(1 - core)) * (2.0 / eps_ref[0])

    kern[...] = p_ref[...] * jnp.exp(dot(pieces(left), (th[...], tl[...]), ((1,), (1,))))

    def settle(x):
        x = x + pltpu.roll(x, 4, 0)
        x = x + pltpu.roll(x, 2, 0)
        return x + pltpu.roll(x, 1, 0)

    def row_total(scale, k, n):
        parts = None
        for j in range(COLS // 128):
            piece = kern[:, j * 128 : (j + 1) * 128]
            if scale is not None:
                piece = piece * scale[0:1, j * 128 : (j + 1) * 128]
            parts = piece if parts is None else parts + piece
        across = parts.T
        x = across[0:8]
        for j in range(1, 16):
            x = x + across[j * 8 : (j + 1) * 8]
        row_in[n, 0] = settle(x)[0:1]
        for d in TGT_ORDER:
            copy(row_in.at[n, 0], row_in.at[n, d], k, TGT[d]).start()
        arrived(row_in.at[n, pl.ds(0, 31)], k)
        x = row_in[n, 0]
        for d in range(1, 32):
            x = x + row_in[n, d]
        return x

    def col_total(down, k, n):
        pieces = []
        for j in range(COLS // 128):
            piece = kern[:, j * 128 : (j + 1) * 128] * down
            x = piece[0:8]
            for i in range(1, 32):
                x = x + piece[i * 8 : (i + 1) * 8]
            pieces.append(settle(x)[0:1])
        col_in[n, si] = jnp.concatenate(pieces, axis=1)
        for d in SRC_ORDER:
            copy(col_in.at[n, si], col_in.at[n, si], k, SRC[d]).start()
        if n == 1:
            for j in range(COLS // 128):
                kern[:, j * 128 : (j + 1) * 128] = kern[:, j * 128 : (j + 1) * 128] * down
        arrived(col_in.at[n, pl.ds(0, 15)], k)
        x = col_in[n, 0]
        for d in range(1, 16):
            x = x + col_in[n, d]
        return x

    scale = None
    for n in range(2):
        row = mass / row_total(scale, 5 + 2 * n, n)
        down = jnp.broadcast_to(row, (128, ROWS)).T
        scale = target / col_total(down, 6 + 2 * n, n)
    col_ref[...] = scale.reshape(COLS)

    kern4 = kern.reshape(16, 2, 8, COLS)
    for k, h in ((0, 1 - core), (1, core)):
        block = kern4[:, h].reshape(128, COLS) * scale
        part[k] = dot(pieces(block), (th[...], tl[...])).reshape(16, 8, D)
        if k == 0:
            copy(part.at[0], part_in, 9, PAIR).start()
    arrived(part_in, 9)
    mine[...] = part[1] + part_in[...]
    for d in TILE_ORDER:
        copy(mine.at[flipped(tile, tileb, d)], last_in.at[d - 1], 10, TILE[d]).start()
    arrived(last_in, 10)
    total = mine[tile]
    for d in range(15):
        total = total + last_in[d]
    own = adown[pl.ds(pl.multiple_of(ti * 8, 8), 8), :]
    for j in range(D // 128):
        out_ref[:, j * 128 : (j + 1) * 128] = total[:, j * 128 : (j + 1) * 128] / own

    for ref, k in pending:
        copy(ref, ref, k, PAIR).wait_send()


def leave(out_in, core_in, col_in, out_ref, core_ref, col_ref, sem):
    pairs = ((core_in, core_ref), (out_in, out_ref), (col_in, col_ref))
    copies = [pltpu.make_async_copy(src, dst, sem.at[k]) for k, (src, dst) in enumerate(pairs)]
    for one in copies:
        one.start()
    for one in copies:
        one.wait()


def per_device(*args):
    f32 = jnp.float32
    vmem = pl.BlockSpec(memory_space=pltpu.VMEM)
    hbm = pl.BlockSpec(memory_space=pltpu.HBM)
    results = (
        jax.ShapeDtypeStruct((8, D), f32),
        jax.ShapeDtypeStruct((D, D), f32),
        jax.ShapeDtypeStruct((COLS,), f32),
    )
    out, core, col = pl.pallas_call(
        body,
        out_shape=results,
        in_specs=[hbm] * 6,
        out_specs=(vmem, vmem, vmem),
        scratch_shapes=[
            pltpu.VMEM((ROWS, D), f32),
            pltpu.VMEM((COLS, D), f32),
            pltpu.VMEM((ROWS, COLS), f32),
            pltpu.VMEM((ROWS,), f32),
            pltpu.VMEM((COLS,), f32),
            pltpu.SMEM((1,), f32),
            pltpu.VMEM((D, ROWS), jnp.bfloat16),
            pltpu.VMEM((D, ROWS), jnp.bfloat16),
            pltpu.VMEM((COLS, D), jnp.bfloat16),
            pltpu.VMEM((COLS, D), jnp.bfloat16),
            pltpu.VMEM((2, 16, SLAB, 128), f32),
            pltpu.VMEM((16, SLAB, 128), f32),
            pltpu.VMEM((16, SLAB, 128), f32),
            pltpu.VMEM((15, SLAB, 128), f32),
            pltpu.VMEM((16, SLAB, 128), f32),
            pltpu.VMEM((2, 16, SLAB, 128), f32),
            pltpu.VMEM((ROWS, COLS), f32),
            pltpu.VMEM((ROWS, 128), f32),
            pltpu.VMEM((2, 32, 1, ROWS), f32),
            pltpu.VMEM((2, 16, 1, COLS), f32),
            pltpu.VMEM((2, 16, 8, D), f32),
            pltpu.VMEM((16, 8, D), f32),
            pltpu.VMEM((16, 8, D), f32),
            pltpu.VMEM((15, 8, D), f32),
            pltpu.SemaphoreType.DMA((10,)),
            pltpu.SemaphoreType.DMA((12,)),
            pltpu.SemaphoreType.DMA((12,)),
        ],
        compiler_params=pltpu.CompilerParams(
            collective_id=0, has_side_effects=True, vmem_limit_bytes=40 * 2**20
        ),
    )(*[pltpu.with_memory_space_constraint(x, pltpu.HBM) for x in args[:5]], args[5])
    out, core, col = pl.pallas_call(
        leave,
        out_shape=results,
        in_specs=[vmem] * 3,
        out_specs=(hbm, hbm, hbm),
        scratch_shapes=[pltpu.SemaphoreType.DMA((3,))],
        compiler_params=pltpu.CompilerParams(vmem_limit_bytes=2**20),
    )(out, core, col)
    return out, core, col


def solution(mesh):
    return jax.shard_map(
        per_device,
        mesh=mesh,
        in_specs=(P("src", None), P("tgt", None), P("src", "tgt"), P("src"), P("tgt"), P()),
        out_specs=(P(("src", "tgt"), None), P(), P("tgt")),
        check_vma=False,
    )
```
